128 devices in a mesh: blk: 16 (over x, y_hi, core), tile: 8 (over z, y_lo).
Axes of the slice: x: 4, y: 4 (y_hi: 2, y_lo: 2; y = y_hi * 2 + y_lo), z: 4, core: 2. Of those that a mesh axis runs over, the one named last changes fastest.
Arguments:
- residual_traces: bfloat16 [131072, 2048], P(('blk', 'tile')), may hold values from -6 to 6
- time_weights: bfloat16 [1024, 2048, 128], P(('blk', 'tile')), may hold values from -0.125 to 0.125
- lateral_amplitude: bfloat16 [1024, 128, 1024], P(('blk', 'tile')), may hold values from -0.1875 to 0.1875
- intersection_tile: int32 [1024, 1], P(('blk', 'tile')), may hold values from 0 to 7; in each aligned block of 8 rows (0 to 7, 8 to 15, ...) at most 2 rows name the same one
- visit_stop: int32 [1024], P(('blk', 'tile')), may hold values from 0 to 3
Outputs:
- image_tiles: float32 [16384, 128], P(('blk', 'tile'))
The draws below stay inside these ranges and needn't reach their ends.
Inputs may be any that keep to these rules, and one draw needn't show every extreme that they name: `intersection_tile`: of the 8 table blocks of one device, at most 2 name the same tile; in every draw some device has 2 blocks naming one tile.
All inputs are finite; a program needn't handle non-finite values.
Results may differ from the reference program's by a relative error of at most 0.0029.
Values may be sent and summed in bfloat16 or wider, within the bound.
A program may use at most 128 MiB of HBM per device.

```python
import math
import jax
import jax.numpy as jnp
import numpy as np
from jax import lax

NS = 2048
NT = 1024
DEPTH = 128
LAT = 128
NB_DEV = 8
MOST = 2
STOPS = 4
TILES = 8
BLOCKS = 1024
TRACES = 131072
N_BLK = 16
N_TILE = 8
DEVICES = 128


def with_ends(entries, rng, low, top_value):
    longest = entries.shape.index(max(entries.shape))
    spots = []
    for shift in (0, 1):
        where = [jax.random.randint(jax.random.fold_in(rng, axis), (), 0, length) for axis, length in enumerate(entries.shape)]
        where[longest] = (where[longest] + shift) % entries.shape[longest]
        spots.append(tuple(where))
    return entries.at[spots[0]].set(low).at[spots[1]].set(top_value)


def level_of(own_key, shape, pieces, least, top_value):
    def one(dim, shards_of):
        heights = jax.random.uniform(jax.random.fold_in(jax.random.fold_in(own_key, 6), dim), (shards_of,), jnp.float32, least / len(pieces), top_value / len(pieces))
        return jnp.repeat(jnp.exp(heights), shape[dim] // shards_of).reshape((-1,) + (1,) * (len(shape) - dim - 1))

    level = one(*pieces[0])
    for cut in pieces[1:]:
        level = level * one(*cut)
    return level


def deal_out(key, own, number, rows, number_of, top, limit, skew):
    order = jax.random.permutation(key, number_of)
    heavy_load, common = load_shares(number_of, rows * top, limit, skew, True), load_shares(number_of, rows * top, limit, skew, False)
    places = jnp.arange(number_of)

    def named(tallies, rotation):
        used = int((tallies > 0).sum())
        fixed = max(1, used // 4)
        passed = fixed + (places - fixed + rotation * (used - fixed)) % max(1, number_of - fixed)
        return jnp.zeros((number_of,), jnp.int32).at[order[jnp.where(places < fixed, places, passed)]].set(jnp.asarray(tallies, jnp.int32))

    tallies = jnp.where(number % 4 == 0, named(heavy_load, number // 4), named(common, number - number // 4 - 1))
    mixed = jax.random.permutation(jax.random.fold_in(own, 3), number_of)
    giver, receiver = mixed[0:number_of // 2 * 2:2], mixed[1:number_of // 2 * 2:2]
    slack = jnp.minimum(tallies[giver] - 1, limit - tallies[receiver]) // 2
    slack = jnp.where((giver == order[0]) | (receiver == order[0]) | (tallies[receiver] == 0), 0, jnp.maximum(slack, 0))
    passed = jax.random.randint(jax.random.fold_in(own, 4), (number_of // 2,), 0, 1 << 20) % (slack + 1)
    tallies = tallies.at[giver].add(-passed).at[receiver].add(passed)
    items = jnp.searchsorted(jnp.cumsum(tallies), jnp.arange(rows * top), side="right").astype(jnp.int32)
    table = items.reshape(top, rows).T
    table = table[jax.random.permutation(jax.random.fold_in(own, 1), rows)]
    rotation = jax.random.randint(jax.random.fold_in(own, 2), (rows, 1), 0, top)
    return jnp.take_along_axis(table, (jnp.arange(top)[None, :] + rotation) % top, axis=1)


def load_shares(count, total, reach, skew, full):
    portions = [(1 << 20) // math.isqrt(grade ** skew) + 1 for grade in range(1, count + 1)]
    largest = reach if full else min(reach, max(-(-total // count), total * portions[0] // sum(portions)))
    least = 1 if total - largest >= count - 1 else 0
    counts, surplus = [largest] + [least] * (count - 1), total - largest - least * (count - 1)
    while surplus > 0:
        free = [i for i in range(1, count) if counts[i] < largest] or [i for i in range(1, count) if counts[i] < reach]
        whole, left = sum([portions[i] for i in free]), surplus
        for i in free:
            addition = min(reach - counts[i], max(1, left * portions[i] // whole), surplus)
            counts[i] = counts[i] + addition
            surplus = surplus - addition
    return np.array(counts)


def centred(own_key, extent, deviation, bound, pieces=(), kind=jnp.bfloat16):
    array = jax.random.normal(own_key, extent, jnp.float32) * deviation
    if len(pieces) > 0:
        array = level_of(own_key, extent, pieces, -0.22, 0.18) * array
    return jnp.clip(array, min=-bound, max=bound).astype(kind)


def setup_inputs(seed: int = 0) -> dict:
    seeds = jax.random.split(jax.random.key(seed), 6)
    residual_traces = centred(seeds[0], (TRACES, NS), 1.0, 6.0, ((0, 128),))
    time_weights = centred(seeds[1], (BLOCKS, NS, DEPTH), NS ** -0.5, 0.125, ((0, 128),))
    lateral_amplitude = centred(seeds[2], (BLOCKS, LAT, NT), NT ** -0.5, 0.1875, ((0, 128),))
    intersection_tile_keys = jax.random.split(jax.random.fold_in(seeds[3], 1), BLOCKS // NB_DEV)
    intersection_tile_turns = jax.random.permutation(jax.random.fold_in(seeds[3], 3), BLOCKS // NB_DEV)
    intersection_tile = jax.vmap(lambda own, number: deal_out(jax.random.fold_in(seeds[3], 2), own, number, NB_DEV, TILES, 1, MOST, 2))(intersection_tile_keys, intersection_tile_turns).reshape((BLOCKS, 1))
    visit_stop = with_ends(jax.random.randint(seeds[4], (BLOCKS,), 0, STOPS), jax.random.fold_in(seeds[4], 1), 0, STOPS - 1).astype(jnp.int32)
    return dict(residual_traces=residual_traces, time_weights=time_weights, lateral_amplitude=lateral_amplitude, intersection_tile=intersection_tile, visit_stop=visit_stop)


def reference(residual_traces, time_weights, lateral_amplitude, intersection_tile, visit_stop):
    traces_dev = residual_traces.reshape(DEVICES, NT, NS)

    def spray(image_sum, inputs):
        weight, amplitude, target, stop_index, block_index = inputs
        source = block_index // NB_DEV
        group_index = source // N_TILE
        owner_dev = group_index * N_TILE + target
        visited = ((group_index - stop_index) % N_BLK) * N_TILE + target
        trace_block = lax.dynamic_index_in_dim(traces_dev, visited, 0, keepdims=False)
        projected = jnp.dot(trace_block, weight, preferred_element_type=jnp.float32).astype(jnp.bfloat16)
        contrib = jnp.dot(amplitude, projected, preferred_element_type=jnp.float32)
        return image_sum.at[owner_dev].add(contrib), None

    image_sum = jnp.zeros((DEVICES, LAT, DEPTH), jnp.float32)
    indices = jnp.arange(BLOCKS, dtype=jnp.int32)
    image_sum, _ = lax.scan(spray, image_sum, (time_weights, lateral_amplitude, intersection_tile[:, 0], visit_stop, indices))
    return image_sum.reshape(DEVICES * LAT, DEPTH)
```

```python
import jax
import jax.numpy as jnp
from jax import lax
from jax.experimental import pallas as pl
from jax.experimental.pallas import tpu as pltpu
from jax.sharding import PartitionSpec as P

MESH = pl.DeviceIdType.MESH
MOST = 2
STOPS = 4
UPPER = 64
PIECES = 4
OFFSETS = (2, 1, 3)
CHUNK = 256
F32 = jnp.float32
BF16 = jnp.bfloat16


def kernel(r_hbm, w_hbm, a_hbm, tile_ref, stop_ref, out_ref, r_all, a_own, w_own, a_pair, w_pair, sa_own, sw_own, sa_pair,
           sw_pair, d_a, d_w, d_info, s_own, s_all, acc, part, loc, info_s, info_r, r_s, r_r, az_s, az_r, wz_s, wz_r,
           ap_s, ap_r, wp_s, wp_r, apz_s, apz_r, wpz_s, wpz_r, al_s, al_r, o_s, o_r):
    blk, tile = lax.axis_index("blk"), lax.axis_index("tile")
    groups, tiles = lax.axis_size("blk"), lax.axis_size("tile")
    zs = tiles // 2
    core, yh = blk % 2, (blk // 2) % 2
    z, h = tile // 2, tile % 2
    label = (h + yh) % 2
    blocks, lat = a_own.shape[0], a_own.shape[1]
    half = w_own.shape[1]
    rows = half // PIECES
    mine = pl.ds(pl.multiple_of(label * half, half), half)
    other = pl.ds(pl.multiple_of((1 - label) * half, half), half)

    pair = (blk, z * 2 + 1 - h)
    sibling = (blk + 1 - 2 * core, tile)
    next_chip = ((blk + 2) % groups, z * 2 + 1 - h)
    after_next = ((blk + 3) % groups, tile)
    drop = ((blk + groups - 1) % groups, z * 2 + 1 - h)
    is_b = (yh * core) == 0
    is_c = core == 1
    is_d = (yh * (1 - core)) == 1

    def remote(src, dst, send, recv, where):
        return pltpu.make_async_remote_copy(src_ref=src, dst_ref=dst, send_sem=send, recv_sem=recv, device_id=where,
                                            device_id_type=MESH)

    def lane_of(d):
        return (blk, ((z + d) % zs) * 2 + h)

    barrier = pltpu.get_barrier_semaphore()

    def greet(where):
        pl.semaphore_signal(barrier, inc=1, device_id=where, device_id_type=MESH)

    for j in range(1, 8):
        greet((blk, (tile + j) % tiles))
    greet(sibling)
    from_yh0_odd = (yh == 0) & (core == 1)

    @pl.when(from_yh0_odd)
    def _():
        greet(((blk + 1) % groups, z * 2 + 1 - h))

    @pl.when(jnp.logical_not(from_yh0_odd))
    def _():
        greet(((blk + groups - 2) % groups, z * 2 + 1 - h))

    @pl.when(core == 0)
    def _():
        greet(((blk + groups - 3) % groups, tile))

    lane = lax.broadcasted_iota(jnp.int32, d_info.shape[1:], 1)
    line = lax.broadcasted_iota(jnp.int32, d_info.shape[1:], 0)
    info = jnp.zeros(d_info.shape[1:], jnp.int32)
    targets = [tile_ref[b, 0] for b in range(blocks)]
    for b in range(blocks):
        rank = sum([(targets[e] == targets[b]).astype(jnp.int32) for e in range(b)], jnp.int32(0))
        value = jnp.where(line == 0, b, jnp.where(line == 1, stop_ref[b], 1))
        info = jnp.where(lane == targets[b] * MOST + rank, value, info)
    d_info[tile] = info

    cp_own = pltpu.make_async_copy(d_info.at[tile], s_own, loc.at[0])
    cp_own.start()
    cp_r = pltpu.make_async_copy(r_hbm.at[:, mine], r_all.at[h, 0], loc.at[1])
    cp_a = pltpu.make_async_copy(a_hbm, a_own, loc.at[2])
    cp_w = pltpu.make_async_copy(w_hbm.at[:, mine, :], w_own, loc.at[3])
    cp_r.start()
    cp_a.start()
    cp_w.start()

    pl.semaphore_wait(barrier, 8 + (1 - yh * core) + core + yh * (1 - core))

    def info_copy(j):
        return remote(d_info.at[tile], d_info.at[tile], info_s.at[j], info_r.at[j], (blk, (tile + j) % tiles))

    for j in range(1, 8):
        info_copy(j).start()

    r_pair = remote(r_hbm.at[:, other], r_all.at[h, 0], r_s.at[0, 0], r_r.at[h, 0], pair)
    a_over = remote(a_hbm.at[:, 0:UPPER, :], a_pair, ap_s.at[0], ap_r.at[0], pair)

    def w_over(i):
        at = pl.ds(pl.multiple_of((1 - label) * half + i * rows, rows), rows)
        return remote(w_hbm.at[:, at, :], w_pair[i], wp_s.at[i], wp_r.at[i], pair)

    r_pair.start()
    a_over.start()
    for i in range(PIECES):
        w_over(i).start()

    def hop(op, j, tau, k_from, k_to, where):
        return remote(r_all.at[tau, k_from], r_all.at[tau, k_to], r_s.at[op, j], r_r.at[tau, k_to], where)

    def taus(j):
        return h if j == 0 else 1 - h

    def op_a(j):
        return hop(1, j, taus(j), 0, 1, sibling)

    def op_b(j):
        return hop(2, j, taus(j), 0, 2, next_chip)

    def op_c(j):
        return hop(3, j, taus(j), 0, 3, after_next)

    def op_d(j):
        return hop(4, j, taus(j), 3, 2, drop)

    def op_e0(j):
        return hop(5, j, taus(j), 2, 3, sibling)

    def op_e1(j):
        return hop(5, j, taus(j), 2, 1, sibling)

    def got_r(tau, k):
        remote(r_all.at[tau, k], r_all.at[tau, k], r_s.at[0, 0], r_r.at[tau, k], pair).wait_recv()

    def spread(j):
        @pl.when(is_c)
        def _():
            op_c(j).start()

        @pl.when(is_b)
        def _():
            op_b(j).start()

        @pl.when(core == 0)
        def _():
            op_a(j).start()

    def forward(j):
        got_r(taus(j), 2)

        @pl.when(core == 0)
        def _():
            op_e0(j).start()

        @pl.when(core == 1)
        def _():
            op_e1(j).start()

    def arrive_3(j):
        got_r(taus(j), 3)

        @pl.when(is_d)
        def _():
            op_d(j).start()

    cp_r.wait()
    spread(0)

    src_me = tile
    src_pair = z * 2 + 1 - h

    def pack(table, count, base, load, store):
        def one(r, carry):
            store(r, load(table(base + r)))
            return carry

        lax.fori_loop(0, count, one, 0)

    def own_block(slot):
        return s_own[0, slot]

    def pair_block(slot):
        return s_all[src_pair, 0, slot]

    def base_of(d):
        return ((z + d) % zs) * (2 * MOST)

    def a_out(d):
        return remote(sa_own.at[d - 1], d_a.at[src_me], az_s.at[d - 1], az_r.at[d - 1], lane_of(d))

    def w_out(d):
        return remote(sw_own.at[d - 1], d_w.at[src_me], wz_s.at[d - 1], wz_r.at[d - 1], lane_of(d))

    cp_own.wait()
    cp_a.wait()
    for d in OFFSETS:
        def put(r, value, d=d):
            sa_own[d - 1, r] = value

        pack(own_block, 4, base_of(d), lambda b: a_own[b], put)
        a_out(d).start()

    def put_a(r, value):
        d_a[src_me, r] = value

    pack(own_block, 4, base_of(0), lambda b: a_own[b], put_a)

    def low(d):
        src = ((z + zs - d) % zs) * 2 + h
        return remote(d_a.at[src, :, UPPER:lat, :], d_a.at[src, :, UPPER:lat, :], al_s.at[d], al_r.at[d], pair)

    low(0).start()
    cp_w.wait()
    for d in OFFSETS:
        def put(r, value, d=d):
            sw_own[d - 1, r] = value

        pack(own_block, 4, base_of(d), lambda b: w_own[b], put)
        w_out(d).start()

    def put_w(r, value):
        d_w[src_me, r] = value

    pack(own_block, 4, base_of(0), lambda b: w_own[b], put_w)

    for j in range(1, 8):
        src = (tile + tiles - j) % tiles
        remote(d_info.at[src], d_info.at[src], info_s.at[j], info_r.at[j], pair).wait_recv()
    cp_all = pltpu.make_async_copy(d_info, s_all, loc.at[4])
    cp_all.start()
    cp_all.wait()

    got_r(1 - h, 0)
    spread(1)

    def ap_out(d):
        return remote(sa_pair.at[d - 1], d_a.at[src_pair, :, 0:UPPER, :], apz_s.at[d - 1], apz_r.at[d - 1], lane_of(d))

    def wp_out(i, d):
        return remote(sw_pair.at[i, d - 1], d_w.at[src_pair, :, pl.ds(i * rows, rows), :], wpz_s.at[i, d - 1],
                      wpz_r.at[i, d - 1], lane_of(d))

    a_over.wait_recv()
    for d in OFFSETS:
        def put(r, value, d=d):
            sa_pair[d - 1, r] = value

        pack(pair_block, 4, base_of(d), lambda b: a_pair[b], put)
        ap_out(d).start()

    def put_ap(r, value):
        d_a[src_pair, r, 0:UPPER, :] = value

    pack(pair_block, 4, base_of(0), lambda b: a_pair[b], put_ap)

    def relay_piece(i):
        w_over(i).wait_recv()
        for d in OFFSETS:
            def put(r, value, d=d):
                sw_pair[i, d - 1, r] = value

            pack(pair_block, 4, base_of(d), lambda b: w_pair[i][b], put)
            wp_out(i, d).start()

        def put_wp(r, value):
            d_w[src_pair, r, i * rows:(i + 1) * rows, :] = value

        pack(pair_block, 4, base_of(0), lambda b: w_pair[i][b], put_wp)

    def source(d, flip):
        return ((z + zs - d) % zs) * 2 + (1 - h if flip else h)

    def got_own_a(d):
        src = source(d, False)
        remote(d_a.at[src], d_a.at[src], az_s.at[d - 1], az_r.at[d - 1], pair).wait_recv()

    for d in (1, 3, 2):
        got_own_a(d)
        low(d).start()

    @pl.when(core == 0)
    def _():
        arrive_3(0)

    forward(1)
    relay_piece(0)
    relay_piece(1)

    @pl.when(core == 0)
    def _():
        arrive_3(1)

    forward(0)
    relay_piece(2)
    relay_piece(3)

    got_r(0, 1)
    got_r(1, 1)

    @pl.when(core == 1)
    def _():
        got_r(0, 3)
        got_r(1, 3)

    acc[...] = jnp.zeros_like(acc)
    first = z * (2 * MOST)

    def facts(src, r):
        return s_all[src, 1, first + r], s_all[src, 2, first + r].astype(F32)

    def chunk_q(src, r, k, n):
        return jnp.dot(d_a[src, r], r_all[r // MOST, k, :, n * CHUNK:(n + 1) * CHUNK],
                       preferred_element_type=F32).astype(BF16)

    def whole(src):
        def one(r, carry):
            k, filled = facts(src, r)
            total = jnp.zeros(acc.shape[1:], F32)
            for n in range(half // CHUNK):
                total += jnp.dot(chunk_q(src, r, k, n), d_w[src, r, n * CHUNK:(n + 1) * CHUNK, :],
                                 preferred_element_type=F32)
            acc[r // MOST] += filled * total
            return carry

        lax.fori_loop(0, 2 * MOST, one, 0)

    def front(src, d):
        def one(r, carry):
            k, _ = facts(src, r)
            for n in range(half // CHUNK):
                sa_own[d - 1, r, :, n * CHUNK:(n + 1) * CHUNK] = chunk_q(src, r, k, n)
            return carry

        lax.fori_loop(0, 2 * MOST, one, 0)

    def back(src, d):
        def one(r, carry):
            _, filled = facts(src, r)
            acc[r // MOST] += filled * jnp.dot(sa_own[d - 1, r], d_w[src, r], preferred_element_type=F32)
            return carry

        lax.fori_loop(0, 2 * MOST, one, 0)

    whole(src_me)
    for d in (1, 3, 2):
        src = source(d, False)
        remote(d_w.at[src], d_w.at[src], wz_s.at[d - 1], wz_r.at[d - 1], pair).wait_recv()
        whole(src)

    def got_low(d):
        at = d_a.at[source(d, True), :, UPPER:lat, :]
        remote(at, at, al_s.at[d], al_r.at[d], pair).wait_recv()

    got_low(0)
    whole(src_pair)
    for d in OFFSETS:
        a_out(d).wait_send()
    for d in (1, 3, 2):
        src = source(d, True)
        at = d_a.at[src, :, 0:UPPER, :]
        remote(at, at, apz_s.at[d - 1], apz_r.at[d - 1], pair).wait_recv()
        got_low(d)
        front(src, d)
    for d in (1, 3, 2):
        src = source(d, True)
        for i in range(PIECES):
            at = d_w.at[src, :, pl.ds(i * rows, rows), :]
            remote(at, at, wpz_s.at[i, d - 1], wpz_r.at[i, d - 1], pair).wait_recv()
        back(src, d)

    home = remote(acc.at[1 - h], part, o_s.at[0], o_r.at[0], pair)
    home.start()

    for j in range(1, 8):
        info_copy(j).wait_send()
    r_pair.wait_send()
    a_over.wait_send()
    for i in range(PIECES):
        w_over(i).wait_send()
    for d in OFFSETS:
        w_out(d).wait_send()
        ap_out(d).wait_send()
        for i in range(PIECES):
            wp_out(i, d).wait_send()
    for d in range(4):
        low(d).wait_send()
    for j in range(2):
        @pl.when(is_c)
        def _():
            op_c(j).wait_send()

        @pl.when(is_b)
        def _():
            op_b(j).wait_send()

        @pl.when(is_d)
        def _():
            op_d(j).wait_send()

        @pl.when(core == 0)
        def _():
            op_a(j).wait_send()
            op_e0(j).wait_send()

        @pl.when(core == 1)
        def _():
            op_e1(j).wait_send()

    home.wait()
    out_ref[...] = acc[h] + part[...]


def body(residual_traces, time_weights, lateral_amplitude, intersection_tile, visit_stop):
    traces, samples = residual_traces.shape
    blocks, _, depth = time_weights.shape
    lat = lateral_amplitude.shape[1]
    tiles = lax.axis_size("tile")
    half, slots = samples // 2, 2 * MOST
    rows = half // PIECES
    hops = tiles // 2 - 1
    dma = pltpu.SemaphoreType.DMA
    return pl.pallas_call(
        kernel,
        out_shape=jax.ShapeDtypeStruct((lat, depth), F32),
        in_specs=[pl.BlockSpec(memory_space=pl.ANY)] * 3 + [pl.BlockSpec(memory_space=pltpu.SMEM)] * 2,
        out_specs=pl.BlockSpec(memory_space=pltpu.VMEM),
        scratch_shapes=[
            pltpu.VMEM((2, STOPS, traces, half), BF16),
            pltpu.VMEM((blocks, lat, traces), BF16),
            pltpu.VMEM((blocks, half, depth), BF16),
            pltpu.VMEM((blocks, UPPER, traces), BF16),
            [pltpu.VMEM((blocks, rows, depth), BF16)] * PIECES,
            pltpu.VMEM((hops, slots, lat, traces), BF16),
            pltpu.VMEM((hops, slots, half, depth), BF16),
            pltpu.VMEM((hops, slots, UPPER, traces), BF16),
            pltpu.VMEM((PIECES, hops, slots, rows, depth), BF16),
            pltpu.VMEM((tiles, slots, lat, traces), BF16),
            pltpu.VMEM((tiles, slots, half, depth), BF16),
            pltpu.VMEM((tiles, 8, 128), jnp.int32),
            pltpu.SMEM((8, 128), jnp.int32),
            pltpu.SMEM((tiles, 8, 128), jnp.int32),
            pltpu.VMEM((2, lat, depth), F32),
            pltpu.VMEM((lat, depth), F32),
            dma((5,)), dma((8,)), dma((8,)), dma((6, 2)), dma((2, STOPS)),
            dma((hops,)), dma((hops,)), dma((hops,)), dma((hops,)), dma((1,)), dma((1,)),
            dma((PIECES,)), dma((PIECES,)), dma((hops,)), dma((hops,)), dma((PIECES, hops)), dma((PIECES, hops)),
            dma((4,)), dma((4,)), dma((1,)), dma((1,)),
        ],
        compiler_params=pltpu.CompilerParams(collective_id=0, has_side_effects=True, vmem_limit_bytes=60 << 20),
        cost_estimate=pl.CostEstimate(flops=10 << 30, bytes_accessed=12 << 20, transcendentals=0),
    )(residual_traces, time_weights, lateral_amplitude, intersection_tile, visit_stop)


def solution(mesh):
    assert mesh.shape["blk"] == 16 and mesh.shape["tile"] == 8
    in_specs = (
        P(("blk", "tile"), None),
        P(("blk", "tile"), None, None),
        P(("blk", "tile"), None, None),
        P(("blk", "tile"), None),
        P(("blk", "tile")),
    )
    out_specs = P(("blk", "tile"), None)
    return jax.shard_map(body, mesh=mesh, in_specs=in_specs, out_specs=out_specs, check_vma=False)
```

```python
import jax
import jax.numpy as jnp
from jax import lax
from jax.experimental import pallas as pl
from jax.experimental.pallas import tpu as pltpu
from jax.sharding import PartitionSpec as P

MESH = pl.DeviceIdType.MESH
MOST = 2
STOPS = 4
UPPER = 64
PIECES = 4
OFFSETS = (2, 1, 3)
CHUNK = 512
F32 = jnp.float32
BF16 = jnp.bfloat16


def kernel(r_hbm, w_hbm, a_hbm, tile_ref, stop_ref, out_ref, r_all, a_own, w_own, a_pair, w_pair, sa_own, sw_own, sa_pair,
           sw_pair, d_a, d_w, d_info, s_all, acc, part, loc, info_s, info_r, r_s, r_r, az_s, az_r, wz_s, wz_r,
           ap_s, ap_r, wp_s, wp_r, apz_s, apz_r, wpz_s, wpz_r, al_s, al_r, o_s, o_r):
    blk, tile = lax.axis_index("blk"), lax.axis_index("tile")
    groups, tiles = lax.axis_size("blk"), lax.axis_size("tile")
    zs = tiles // 2
    core, yh = blk % 2, (blk // 2) % 2
    z, h = tile // 2, tile % 2
    label = (h + yh) % 2
    blocks, lat = a_own.shape[0], a_own.shape[1]
    half = w_own.shape[1]
    rows = half // PIECES
    mine = pl.ds(pl.multiple_of(label * half, half), half)
    other = pl.ds(pl.multiple_of((1 - label) * half, half), half)

    pair = (blk, z * 2 + 1 - h)
    sibling = (blk + 1 - 2 * core, tile)
    next_chip = ((blk + 2) % groups, z * 2 + 1 - h)
    after_next = ((blk + 3) % groups, tile)
    drop = ((blk + groups - 1) % groups, z * 2 + 1 - h)
    is_b = (yh * core) == 0
    is_c = core == 1
    is_d = (yh * (1 - core)) == 1

    def remote(src, dst, send, recv, where):
        return pltpu.make_async_remote_copy(src_ref=src, dst_ref=dst, send_sem=send, recv_sem=recv, device_id=where,
                                            device_id_type=MESH)

    def lane_of(d):
        return (blk, ((z + d) % zs) * 2 + h)

    cp_a = pltpu.make_async_copy(a_hbm, a_own, loc.at[0])
    cp_r = pltpu.make_async_copy(r_hbm.at[:, mine], r_all.at[h, 0], loc.at[1])
    cp_w = pltpu.make_async_copy(w_hbm.at[:, mine, :], w_own, loc.at[2])
    cp_a.start()
    cp_r.start()
    cp_w.start()

    barrier = pltpu.get_barrier_semaphore()

    def greet(where):
        pl.semaphore_signal(barrier, inc=1, device_id=where, device_id_type=MESH)

    for j in range(1, 8):
        greet((blk, (tile + j) % tiles))
    greet(sibling)
    from_yh0_odd = (yh == 0) & (core == 1)

    @pl.when(from_yh0_odd)
    def _():
        greet(((blk + 1) % groups, z * 2 + 1 - h))

    @pl.when(jnp.logical_not(from_yh0_odd))
    def _():
        greet(((blk + groups - 2) % groups, z * 2 + 1 - h))

    @pl.when(core == 0)
    def _():
        greet(((blk + groups - 3) % groups, tile))

    lane = lax.broadcasted_iota(jnp.int32, d_info.shape[1:], 1)
    line = lax.broadcasted_iota(jnp.int32, d_info.shape[1:], 0)
    info = jnp.zeros(d_info.shape[1:], jnp.int32)
    targets = [tile_ref[b] for b in range(blocks)]
    slot_of = []
    for b in range(blocks):
        rank = sum([(targets[e] == targets[b]).astype(jnp.int32) for e in range(b)], jnp.int32(0))
        slot_of.append(targets[b] * MOST + rank)
        value = jnp.where(line == 0, b, jnp.where(line == 1, stop_ref[b], 1))
        info = jnp.where(lane == slot_of[b], value, info)
    d_info[tile] = info

    src_me = tile
    src_pair = z * 2 + 1 - h

    def pack(table, count, base, load, store):
        def one(r, carry):
            store(r, load(table(base + r)))
            return carry

        lax.fori_loop(0, count, one, 0)

    def own_block(slot):
        block = jnp.int32(0)
        for b in range(1, blocks):
            block = jnp.where(slot_of[b] == slot, b, block)
        return block

    def pair_block(slot):
        return s_all[src_pair, 0, slot]

    def base_of(d):
        return ((z + d) % zs) * (2 * MOST)

    def a_out(d):
        return remote(sa_own.at[d - 1], d_a.at[src_me], az_s.at[d - 1], az_r.at[d - 1], lane_of(d))

    cp_a.wait()
    for d in OFFSETS:
        def put(r, value, d=d):
            sa_own[d - 1, r] = value

        pack(own_block, 4, base_of(d), lambda b: a_own[b], put)

    pl.semaphore_wait(barrier, 8 + (1 - yh * core) + core + yh * (1 - core))

    def info_copy(j):
        return remote(d_info.at[tile], d_info.at[tile], info_s.at[j], info_r.at[j], (blk, (tile + j) % tiles))

    for j in range(1, 8):
        info_copy(j).start()

    r_pair = remote(r_hbm.at[:, other], r_all.at[h, 0], r_s.at[0, 0], r_r.at[h, 0], pair)
    a_over = remote(a_hbm.at[:, 0:UPPER, :], a_pair, ap_s.at[0], ap_r.at[0], pair)

    def w_over(i):
        at = pl.ds(pl.multiple_of((1 - label) * half + i * rows, rows), rows)
        return remote(w_hbm.at[:, at, :], w_pair[i], wp_s.at[i], wp_r.at[i], pair)

    r_pair.start()
    for d in OFFSETS:
        a_out(d).start()
    a_over.start()
    for i in range(PIECES):
        w_over(i).start()

    def hop(op, j, tau, k_from, k_to, where):
        return remote(r_all.at[tau, k_from], r_all.at[tau, k_to], r_s.at[op, j], r_r.at[tau, k_to], where)

    def taus(j):
        return h if j == 0 else 1 - h

    def op_a(j):
        return hop(1, j, taus(j), 0, 1, sibling)

    def op_b(j):
        return hop(2, j, taus(j), 0, 2, next_chip)

    def op_c(j):
        return hop(3, j, taus(j), 0, 3, after_next)

    def op_d(j):
        return hop(4, j, taus(j), 3, 2, drop)

    def op_e0(j):
        return hop(5, j, taus(j), 2, 3, sibling)

    def op_e1(j):
        return hop(5, j, taus(j), 2, 1, sibling)

    def got_r(tau, k):
        remote(r_all.at[tau, k], r_all.at[tau, k], r_s.at[0, 0], r_r.at[tau, k], pair).wait_recv()

    def spread(j):
        @pl.when(is_c)
        def _():
            op_c(j).start()

        @pl.when(is_b)
        def _():
            op_b(j).start()

        @pl.when(core == 0)
        def _():
            op_a(j).start()

    def forward(j):
        got_r(taus(j), 2)

        @pl.when(core == 0)
        def _():
            op_e0(j).start()

        @pl.when(core == 1)
        def _():
            op_e1(j).start()

    def arrive_3(j):
        got_r(taus(j), 3)

        @pl.when(is_d)
        def _():
            op_d(j).start()

    cp_r.wait()
    spread(0)

    def w_out(d):
        return remote(sw_own.at[d - 1], d_w.at[src_me], wz_s.at[d - 1], wz_r.at[d - 1], lane_of(d))

    def put_a(r, value):
        d_a[src_me, r] = value

    pack(own_block, 4, base_of(0), lambda b: a_own[b], put_a)

    def source(d, flip):
        return ((z + zs - d) % zs) * 2 + (1 - h if flip else h)

    def low_at(src, tau):
        return d_a.at[src, pl.ds(tau * MOST, MOST), UPPER:lat, :]

    def low(d, t):
        at = low_at(source(d, False), h if t == 0 else 1 - h)
        return remote(at, at, al_s.at[d, t], al_r.at[d, t], pair)

    cp_w.wait()
    for d in OFFSETS:
        def put(r, value, d=d):
            sw_own[d - 1, r] = value

        pack(own_block, 4, base_of(d), lambda b: w_own[b], put)
        w_out(d).start()

    def put_w(r, value):
        d_w[src_me, r] = value

    pack(own_block, 4, base_of(0), lambda b: w_own[b], put_w)

    for j in range(1, 8):
        src = (tile + tiles - j) % tiles
        remote(d_info.at[src], d_info.at[src], info_s.at[j], info_r.at[j], pair).wait_recv()
    cp_all = pltpu.make_async_copy(d_info, s_all, loc.at[3])
    cp_all.start()
    cp_all.wait()

    got_r(1 - h, 0)
    spread(1)

    def ap_out(d):
        return remote(sa_pair.at[d - 1], d_a.at[src_pair, :, 0:UPPER, :], apz_s.at[d - 1], apz_r.at[d - 1], lane_of(d))

    def wp_out(i, d, t):
        two = pl.ds((1 - h if t == 0 else h) * MOST, MOST)
        return remote(sw_pair.at[i, d - 1, two], d_w.at[src_pair, two, pl.ds(i * rows, rows), :], wpz_s.at[i, d - 1, t],
                      wpz_r.at[i, d - 1, t], lane_of(d))

    a_over.wait_recv()
    for d in OFFSETS:
        def put(r, value, d=d):
            sa_pair[d - 1, r] = value

        pack(pair_block, 4, base_of(d), lambda b: a_pair[b], put)
        ap_out(d).start()

    def put_ap(r, value):
        d_a[src_pair, r, 0:UPPER, :] = value

    pack(pair_block, 4, base_of(0), lambda b: a_pair[b], put_ap)

    def relay_piece(i, t):
        skip = (1 - h if t == 0 else h) * MOST
        for d in OFFSETS:
            def put(r, value, d=d):
                sw_pair[i, d - 1, skip + r] = value

            pack(pair_block, MOST, base_of(d) + skip, lambda b: w_pair[i][b], put)
            wp_out(i, d, t).start()

        def put_wp(r, value):
            d_w[src_pair, skip + r, i * rows:(i + 1) * rows, :] = value

        pack(pair_block, MOST, base_of(0) + skip, lambda b: w_pair[i][b], put_wp)

    def got_own_a(d):
        src = source(d, False)
        remote(d_a.at[src], d_a.at[src], az_s.at[d - 1], az_r.at[d - 1], pair).wait_recv()

    for d in (1, 3, 2):
        got_own_a(d)
    for t in range(2):
        for d in range(4):
            low(d, t).start()

    @pl.when(core == 0)
    def _():
        arrive_3(0)

    forward(1)
    w_over(0).wait_recv()
    relay_piece(0, 0)
    w_over(1).wait_recv()
    relay_piece(1, 0)

    @pl.when(core == 0)
    def _():
        arrive_3(1)

    w_over(2).wait_recv()
    relay_piece(2, 0)
    w_over(3).wait_recv()
    relay_piece(3, 0)
    for i in range(PIECES):
        relay_piece(i, 1)
    forward(0)

    got_r(0, 1)
    got_r(1, 1)

    @pl.when(core == 1)
    def _():
        got_r(0, 3)
        got_r(1, 3)

    acc[...] = jnp.zeros_like(acc)
    first = z * (2 * MOST)

    def facts(src, r):
        return s_all[src, 1, first + r], s_all[src, 2, first + r].astype(F32)

    def chunk_q(src, r, k, n):
        return jnp.dot(d_a[src, r], r_all[r // MOST, k, :, n * CHUNK:(n + 1) * CHUNK],
                       preferred_element_type=F32).astype(BF16)

    def whole(src, begin, count):
        def one(r, carry):
            k, filled = facts(src, r)
            total = jnp.zeros(acc.shape[1:], F32)
            for n in range(half // CHUNK):
                total += jnp.dot(chunk_q(src, r, k, n), d_w[src, r, n * CHUNK:(n + 1) * CHUNK, :],
                                 preferred_element_type=F32)
            acc[r // MOST] += filled * total
            return carry

        lax.fori_loop(begin, begin + count, one, 0)

    def front(src, d, begin):
        def one(r, carry):
            k, _ = facts(src, r)
            for n in range(half // CHUNK):
                sa_own[d - 1, r, :, n * CHUNK:(n + 1) * CHUNK] = chunk_q(src, r, k, n)
            return carry

        lax.fori_loop(begin, begin + MOST, one, 0)

    def back(src, d, begin, low_row, high_row):
        def one(r, carry):
            _, filled = facts(src, r)
            acc[r // MOST] += filled * jnp.dot(sa_own[d - 1, r, :, low_row:high_row], d_w[src, r, low_row:high_row, :],
                                               preferred_element_type=F32)
            return carry

        lax.fori_loop(begin, begin + MOST, one, 0)

    whole(src_me, 0, 2 * MOST)
    for d in (1, 3, 2):
        src = source(d, False)
        remote(d_w.at[src], d_w.at[src], wz_s.at[d - 1], wz_r.at[d - 1], pair).wait_recv()
        whole(src, 0, 2 * MOST)
    for d in OFFSETS:
        a_out(d).wait_send()
    for d in OFFSETS:
        at = d_a.at[source(d, True), :, 0:UPPER, :]
        remote(at, at, apz_s.at[d - 1], apz_r.at[d - 1], pair).wait_recv()

    home = remote(acc.at[1 - h], part, o_s.at[0], o_r.at[0], pair)
    last = half - rows
    for t in range(2):
        tau = 1 - h if t == 0 else h
        begin = tau * MOST

        def got_low(d):
            at = low_at(source(d, True), tau)
            remote(at, at, al_s.at[d, t], al_r.at[d, t], pair).wait_recv()

        def got_w(d, i):
            at = d_w.at[source(d, True), pl.ds(begin, MOST), pl.ds(i * rows, rows), :]
            remote(at, at, wpz_s.at[i, d - 1, t], wpz_r.at[i, d - 1, t], pair).wait_recv()

        got_low(0)
        whole(src_pair, begin, MOST)
        for d in (1, 2, 3):
            got_low(d)
            front(source(d, True), d, begin)
        for d in OFFSETS:
            for i in range(PIECES - 1):
                got_w(d, i)
            back(source(d, True), d, begin, 0, last)
        for d in OFFSETS:
            got_w(d, PIECES - 1)
            back(source(d, True), d, begin, last, half)
        if t == 0:
            home.start()

    for j in range(1, 8):
        info_copy(j).wait_send()
    r_pair.wait_send()
    a_over.wait_send()
    for i in range(PIECES):
        w_over(i).wait_send()
    for d in OFFSETS:
        w_out(d).wait_send()
        ap_out(d).wait_send()
        for i in range(PIECES):
            for t in range(2):
                wp_out(i, d, t).wait_send()
    for d in range(4):
        for t in range(2):
            low(d, t).wait_send()
    for j in range(2):
        @pl.when(is_c)
        def _():
            op_c(j).wait_send()

        @pl.when(is_b)
        def _():
            op_b(j).wait_send()

        @pl.when(is_d)
        def _():
            op_d(j).wait_send()

        @pl.when(core == 0)
        def _():
            op_a(j).wait_send()
            op_e0(j).wait_send()

        @pl.when(core == 1)
        def _():
            op_e1(j).wait_send()

    home.wait()
    out_ref[...] = acc[h] + part[...]


def body(residual_traces, time_weights, lateral_amplitude, intersection_tile, visit_stop):
    traces, samples = residual_traces.shape
    blocks, _, depth = time_weights.shape
    lat = lateral_amplitude.shape[1]
    tiles = lax.axis_size("tile")
    half, slots = samples // 2, 2 * MOST
    rows = half // PIECES
    hops = tiles // 2 - 1
    dma = pltpu.SemaphoreType.DMA
    return pl.pallas_call(
        kernel,
        out_shape=jax.ShapeDtypeStruct((lat, depth), F32),
        in_specs=[pl.BlockSpec(memory_space=pl.ANY)] * 3 + [pl.BlockSpec(memory_space=pltpu.SMEM)] * 2,
        out_specs=pl.BlockSpec(memory_space=pltpu.VMEM),
        scratch_shapes=[
            pltpu.VMEM((2, STOPS, traces, half), BF16),
            pltpu.VMEM((blocks, lat, traces), BF16),
            pltpu.VMEM((blocks, half, depth), BF16),
            pltpu.VMEM((blocks, UPPER, traces), BF16),
            [pltpu.VMEM((blocks, rows, depth), BF16)] * PIECES,
            pltpu.VMEM((hops, slots, lat, traces), BF16),
            pltpu.VMEM((hops, slots, half, depth), BF16),
            pltpu.VMEM((hops, slots, UPPER, traces), BF16),
            pltpu.VMEM((PIECES, hops, slots, rows, depth), BF16),
            pltpu.VMEM((tiles, slots, lat, traces), BF16),
            pltpu.VMEM((tiles, slots, half, depth), BF16),
            pltpu.VMEM((tiles, 8, 128), jnp.int32),
            pltpu.SMEM((tiles, 8, 128), jnp.int32),
            pltpu.VMEM((2, lat, depth), F32),
            pltpu.VMEM((lat, depth), F32),
            dma((4,)), dma((8,)), dma((8,)), dma((6, 2)), dma((2, STOPS)),
            dma((hops,)), dma((hops,)), dma((hops,)), dma((hops,)), dma((1,)), dma((1,)),
            dma((PIECES,)), dma((PIECES,)), dma((hops,)), dma((hops,)), dma((PIECES, hops, 2)), dma((PIECES, hops, 2)),
            dma((4, 2)), dma((4, 2)), dma((1,)), dma((1,)),
        ],
        compiler_params=pltpu.CompilerParams(collective_id=0, has_side_effects=True, vmem_limit_bytes=60 << 20),
        cost_estimate=pl.CostEstimate(flops=10 << 30, bytes_accessed=12 << 20, transcendentals=0),
    )(residual_traces, time_weights, lateral_amplitude, intersection_tile.reshape(blocks), visit_stop)


def solution(mesh):
    assert mesh.shape["blk"] == 16 and mesh.shape["tile"] == 8
    in_specs = (
        P(("blk", "tile"), None),
        P(("blk", "tile"), None, None),
        P(("blk", "tile"), None, None),
        P(("blk", "tile"), None),
        P(("blk", "tile")),
    )
    out_specs = P(("blk", "tile"), None)
    return jax.shard_map(body, mesh=mesh, in_specs=in_specs, out_specs=out_specs, check_vma=False)
```

```python
import jax
import jax.numpy as jnp
from jax import lax
from jax.experimental import pallas as pl
from jax.experimental.pallas import tpu as pltpu
from jax.sharding import PartitionSpec as P

MESH = pl.DeviceIdType.MESH
MOST = 2
STOPS = 4
UPPER = 64
PIECES = 4
OFFSETS = (2, 1, 3)
CHUNK = 512
F32 = jnp.float32
BF16 = jnp.bfloat16


def kernel(r_hbm, w_hbm, a_hbm, tile_hbm, stop_hbm, out_ref, r_all, a_own, w_own, a_pair, w_pair, sa_own, sw_own, sa_pair,
           sw_pair, d_a, d_w, d_info, tile_ref, stop_ref, s_all, acc, part, loc, info_s, info_r, r_s, r_r, az_s, az_r, wz_s, wz_r,
           ap_s, ap_r, wp_s, wp_r, apz_s, apz_r, wpz_s, wpz_r, al_s, al_r, o_s, o_r):
    blk, tile = lax.axis_index("blk"), lax.axis_index("tile")
    groups, tiles = lax.axis_size("blk"), lax.axis_size("tile")
    zs = tiles // 2
    core, yh = blk % 2, (blk // 2) % 2
    z, h = tile // 2, tile % 2
    label = (h + yh) % 2
    blocks, lat = a_own.shape[0], a_own.shape[1]
    half = w_own.shape[1]
    rows = half // PIECES
    mine = pl.ds(pl.multiple_of(label * half, half), half)
    other = pl.ds(pl.multiple_of((1 - label) * half, half), half)

    pair = (blk, z * 2 + 1 - h)
    sibling = (blk + 1 - 2 * core, tile)
    next_chip = ((blk + 2) % groups, z * 2 + 1 - h)
    after_next = ((blk + 3) % groups, tile)
    drop = ((blk + groups - 1) % groups, z * 2 + 1 - h)
    is_b = (yh * core) == 0
    is_c = core == 1
    is_d = (yh * (1 - core)) == 1

    def remote(src, dst, send, recv, where):
        return pltpu.make_async_remote_copy(src_ref=src, dst_ref=dst, send_sem=send, recv_sem=recv, device_id=where,
                                            device_id_type=MESH)

    def lane_of(d):
        return (blk, ((z + d) % zs) * 2 + h)

    cp_a = pltpu.make_async_copy(a_hbm, a_own, loc.at[0])
    cp_r = pltpu.make_async_copy(r_hbm.at[:, mine], r_all.at[h, 0], loc.at[1])
    cp_w = pltpu.make_async_copy(w_hbm.at[:, mine, :], w_own, loc.at[2])
    cp_tile = pltpu.make_async_copy(tile_hbm, tile_ref, loc.at[4])
    cp_stop = pltpu.make_async_copy(stop_hbm, stop_ref, loc.at[5])
    cp_tile.start()
    cp_stop.start()
    cp_a.start()
    cp_r.start()
    cp_w.start()

    barrier = pltpu.get_barrier_semaphore()

    def greet(where):
        pl.semaphore_signal(barrier, inc=1, device_id=where, device_id_type=MESH)

    for j in range(1, 8):
        greet((blk, (tile + j) % tiles))
    greet(sibling)
    from_yh0_odd = (yh == 0) & (core == 1)

    @pl.when(from_yh0_odd)
    def _():
        greet(((blk + 1) % groups, z * 2 + 1 - h))

    @pl.when(jnp.logical_not(from_yh0_odd))
    def _():
        greet(((blk + groups - 2) % groups, z * 2 + 1 - h))

    @pl.when(core == 0)
    def _():
        greet(((blk + groups - 3) % groups, tile))

    lane = lax.broadcasted_iota(jnp.int32, d_info.shape[1:], 1)
    line = lax.broadcasted_iota(jnp.int32, d_info.shape[1:], 0)
    info = jnp.zeros(d_info.shape[1:], jnp.int32)
    cp_tile.wait()
    cp_stop.wait()
    targets = [tile_ref[b] for b in range(blocks)]
    slot_of = []
    for b in range(blocks):
        rank = sum([(targets[e] == targets[b]).astype(jnp.int32) for e in range(b)], jnp.int32(0))
        slot_of.append(targets[b] * MOST + rank)
        value = jnp.where(line == 0, b, jnp.where(line == 1, stop_ref[b], 1))
        info = jnp.where(lane == slot_of[b], value, info)
    d_info[tile] = info

    src_me = tile
    src_pair = z * 2 + 1 - h

    def pack(table, count, base, load, store):
        def one(r, carry):
            store(r, load(table(base + r)))
            return carry

        lax.fori_loop(0, count, one, 0)

    def own_block(slot):
        block = jnp.int32(0)
        for b in range(1, blocks):
            block = jnp.where(slot_of[b] == slot, b, block)
        return block

    def pair_block(slot):
        return s_all[src_pair, 0, slot]

    def base_of(d):
        return ((z + d) % zs) * (2 * MOST)

    def a_out(d):
        return remote(sa_own.at[d - 1], d_a.at[src_me], az_s.at[d - 1], az_r.at[d - 1], lane_of(d))

    cp_a.wait()
    for d in OFFSETS:
        def put(r, value, d=d):
            sa_own[d - 1, r] = value

        pack(own_block, 4, base_of(d), lambda b: a_own[b], put)

    pl.semaphore_wait(barrier, 8 + (1 - yh * core) + core + yh * (1 - core))

    def info_copy(j):
        return remote(d_info.at[tile], d_info.at[tile], info_s.at[j], info_r.at[j], (blk, (tile + j) % tiles))

    for j in range(1, 8):
        info_copy(j).start()

    r_pair = remote(r_hbm.at[:, other], r_all.at[h, 0], r_s.at[0, 0], r_r.at[h, 0], pair)
    a_over = remote(a_hbm.at[:, 0:UPPER, :], a_pair, ap_s.at[0], ap_r.at[0], pair)

    def w_over(i):
        at = pl.ds(pl.multiple_of((1 - label) * half + i * rows, rows), rows)
        return remote(w_hbm.at[:, at, :], w_pair[i], wp_s.at[i], wp_r.at[i], pair)

    r_pair.start()
    for d in OFFSETS:
        a_out(d).start()
    a_over.start()
    for i in range(PIECES):
        w_over(i).start()

    def hop(op, j, tau, k_from, k_to, where):
        return remote(r_all.at[tau, k_from], r_all.at[tau, k_to], r_s.at[op, j], r_r.at[tau, k_to], where)

    def taus(j):
        return h if j == 0 else 1 - h

    def op_a(j):
        return hop(1, j, taus(j), 0, 1, sibling)

    def op_b(j):
        return hop(2, j, taus(j), 0, 2, next_chip)

    def op_c(j):
        return hop(3, j, taus(j), 0, 3, after_next)

    def op_d(j):
        return hop(4, j, taus(j), 3, 2, drop)

    def op_e0(j):
        return hop(5, j, taus(j), 2, 3, sibling)

    def op_e1(j):
        return hop(5, j, taus(j), 2, 1, sibling)

    def got_r(tau, k):
        remote(r_all.at[tau, k], r_all.at[tau, k], r_s.at[0, 0], r_r.at[tau, k], pair).wait_recv()

    def spread(j):
        @pl.when(is_c)
        def _():
            op_c(j).start()

        @pl.when(is_b)
        def _():
            op_b(j).start()

        @pl.when(core == 0)
        def _():
            op_a(j).start()

    def forward(j):
        got_r(taus(j), 2)

        @pl.when(core == 0)
        def _():
            op_e0(j).start()

        @pl.when(core == 1)
        def _():
            op_e1(j).start()

    def arrive_3(j):
        got_r(taus(j), 3)

        @pl.when(is_d)
        def _():
            op_d(j).start()

    cp_r.wait()
    spread(0)

    def w_out(d):
        return remote(sw_own.at[d - 1], d_w.at[src_me], wz_s.at[d - 1], wz_r.at[d - 1], lane_of(d))

    def put_a(r, value):
        d_a[src_me, r] = value

    pack(own_block, 4, base_of(0), lambda b: a_own[b], put_a)

    def source(d, flip):
        return ((z + zs - d) % zs) * 2 + (1 - h if flip else h)

    def low_at(src, tau):
        return d_a.at[src, pl.ds(tau * MOST, MOST), UPPER:lat, :]

    def low(d, t):
        at = low_at(source(d, False), h if t == 0 else 1 - h)
        return remote(at, at, al_s.at[d, t], al_r.at[d, t], pair)

    cp_w.wait()
    for d in OFFSETS:
        def put(r, value, d=d):
            sw_own[d - 1, r] = value

        pack(own_block, 4, base_of(d), lambda b: w_own[b], put)
        w_out(d).start()

    def put_w(r, value):
        d_w[src_me, r] = value

    pack(own_block, 4, base_of(0), lambda b: w_own[b], put_w)

    for j in range(1, 8):
        src = (tile + tiles - j) % tiles
        remote(d_info.at[src], d_info.at[src], info_s.at[j], info_r.at[j], pair).wait_recv()
    cp_all = pltpu.make_async_copy(d_info, s_all, loc.at[3])
    cp_all.start()
    cp_all.wait()

    got_r(1 - h, 0)
    spread(1)

    def ap_out(d):
        return remote(sa_pair.at[d - 1], d_a.at[src_pair, :, 0:UPPER, :], apz_s.at[d - 1], apz_r.at[d - 1], lane_of(d))

    def wp_out(i, d, t):
        two = pl.ds((1 - h if t == 0 else h) * MOST, MOST)
        return remote(sw_pair.at[i, d - 1, two], d_w.at[src_pair, two, pl.ds(i * rows, rows), :], wpz_s.at[i, d - 1, t],
                      wpz_r.at[i, d - 1, t], lane_of(d))

    a_over.wait_recv()
    for d in OFFSETS:
        def put(r, value, d=d):
            sa_pair[d - 1, r] = value

        pack(pair_block, 4, base_of(d), lambda b: a_pair[b], put)
        ap_out(d).start()

    def put_ap(r, value):
        d_a[src_pair, r, 0:UPPER, :] = value

    pack(pair_block, 4, base_of(0), lambda b: a_pair[b], put_ap)

    def relay_piece(i, t):
        skip = (1 - h if t == 0 else h) * MOST
        for d in OFFSETS:
            def put(r, value, d=d):
                sw_pair[i, d - 1, skip + r] = value

            pack(pair_block, MOST, base_of(d) + skip, lambda b: w_pair[i][b], put)
            wp_out(i, d, t).start()

        def put_wp(r, value):
            d_w[src_pair, skip + r, i * rows:(i + 1) * rows, :] = value

        pack(pair_block, MOST, base_of(0) + skip, lambda b: w_pair[i][b], put_wp)

    def got_own_a(d):
        src = source(d, False)
        remote(d_a.at[src], d_a.at[src], az_s.at[d - 1], az_r.at[d - 1], pair).wait_recv()

    for d in (1, 3, 2):
        got_own_a(d)
    for t in range(2):
        for d in range(4):
            low(d, t).start()

    @pl.when(core == 0)
    def _():
        arrive_3(0)

    forward(1)
    w_over(0).wait_recv()
    relay_piece(0, 0)
    w_over(1).wait_recv()
    relay_piece(1, 0)

    @pl.when(core == 0)
    def _():
        arrive_3(1)

    w_over(2).wait_recv()
    relay_piece(2, 0)
    w_over(3).wait_recv()
    relay_piece(3, 0)
    for i in range(PIECES):
        relay_piece(i, 1)
    forward(0)

    got_r(0, 1)
    got_r(1, 1)

    @pl.when(core == 1)
    def _():
        got_r(0, 3)
        got_r(1, 3)

    acc[...] = jnp.zeros_like(acc)
    first = z * (2 * MOST)

    def facts(src, r):
        return s_all[src, 1, first + r], s_all[src, 2, first + r].astype(F32)

    def chunk_q(src, r, k, n):
        return jnp.dot(d_a[src, r], r_all[r // MOST, k, :, n * CHUNK:(n + 1) * CHUNK],
                       preferred_element_type=F32).astype(BF16)

    def whole(src, begin, count):
        def one(r, carry):
            k, filled = facts(src, r)
            total = jnp.zeros(acc.shape[1:], F32)
            for n in range(half // CHUNK):
                total += jnp.dot(chunk_q(src, r, k, n), d_w[src, r, n * CHUNK:(n + 1) * CHUNK, :],
                                 preferred_element_type=F32)
            acc[r // MOST] += filled * total
            return carry

        lax.fori_loop(begin, begin + count, one, 0)

    def front(src, d, begin):
        def one(r, carry):
            k, _ = facts(src, r)
            for n in range(half // CHUNK):
                sa_own[d - 1, r, :, n * CHUNK:(n + 1) * CHUNK] = chunk_q(src, r, k, n)
            return carry

        lax.fori_loop(begin, begin + MOST, one, 0)

    def back(src, d, begin, low_row, high_row):
        def one(r, carry):
            _, filled = facts(src, r)
            acc[r // MOST] += filled * jnp.dot(sa_own[d - 1, r, :, low_row:high_row], d_w[src, r, low_row:high_row, :],
                                               preferred_element_type=F32)
            return carry

        lax.fori_loop(begin, begin + MOST, one, 0)

    whole(src_me, 0, 2 * MOST)
    for d in (1, 3, 2):
        src = source(d, False)
        remote(d_w.at[src], d_w.at[src], wz_s.at[d - 1], wz_r.at[d - 1], pair).wait_recv()
        whole(src, 0, 2 * MOST)
    for d in OFFSETS:
        a_out(d).wait_send()
    for d in OFFSETS:
        at = d_a.at[source(d, True), :, 0:UPPER, :]
        remote(at, at, apz_s.at[d - 1], apz_r.at[d - 1], pair).wait_recv()

    home = remote(acc.at[1 - h], part, o_s.at[0], o_r.at[0], pair)
    last = half - rows
    for t in range(2):
        tau = 1 - h if t == 0 else h
        begin = tau * MOST

        def got_low(d):
            at = low_at(source(d, True), tau)
            remote(at, at, al_s.at[d, t], al_r.at[d, t], pair).wait_recv()

        def got_w(d, i):
            at = d_w.at[source(d, True), pl.ds(begin, MOST), pl.ds(i * rows, rows), :]
            remote(at, at, wpz_s.at[i, d - 1, t], wpz_r.at[i, d - 1, t], pair).wait_recv()

        got_low(0)
        whole(src_pair, begin, MOST)
        for d in (1, 2, 3):
            got_low(d)
            front(source(d, True), d, begin)
            for i in range(PIECES - 1):
                got_w(d, i)
            back(source(d, True), d, begin, 0, last)
        for d in OFFSETS:
            got_w(d, PIECES - 1)
            back(source(d, True), d, begin, last, half)
        if t == 0:
            home.start()
            for j in range(1, 8):
                info_copy(j).wait_send()
            r_pair.wait_send()
            a_over.wait_send()
            for i in range(PIECES):
                w_over(i).wait_send()
            for d in OFFSETS:
                w_out(d).wait_send()
                ap_out(d).wait_send()
                for i in range(PIECES):
                    wp_out(i, d, 0).wait_send()
            for d in range(4):
                low(d, 0).wait_send()
            for j in range(2):
                @pl.when(is_c)
                def _():
                    op_c(j).wait_send()

                @pl.when(is_b)
                def _():
                    op_b(j).wait_send()

                @pl.when(is_d)
                def _():
                    op_d(j).wait_send()

                @pl.when(core == 0)
                def _():
                    op_a(j).wait_send()
                    op_e0(j).wait_send()

                @pl.when(core == 1)
                def _():
                    op_e1(j).wait_send()


    for d in OFFSETS:
        for i in range(PIECES):
            wp_out(i, d, 1).wait_send()
    for d in range(4):
        low(d, 1).wait_send()
    home.wait()
    out_ref[...] = acc[h] + part[...]


def body(residual_traces, time_weights, lateral_amplitude, intersection_tile, visit_stop):
    traces, samples = residual_traces.shape
    blocks, _, depth = time_weights.shape
    lat = lateral_amplitude.shape[1]
    tiles = lax.axis_size("tile")
    half, slots = samples // 2, 2 * MOST
    rows = half // PIECES
    hops = tiles // 2 - 1
    dma = pltpu.SemaphoreType.DMA
    return pl.pallas_call(
        kernel,
        out_shape=jax.ShapeDtypeStruct((lat, depth), F32),
        in_specs=[pl.BlockSpec(memory_space=pl.ANY)] * 5,
        out_specs=pl.BlockSpec(memory_space=pltpu.VMEM),
        scratch_shapes=[
            pltpu.VMEM((2, STOPS, traces, half), BF16),
            pltpu.VMEM((blocks, lat, traces), BF16),
            pltpu.VMEM((blocks, half, depth), BF16),
            pltpu.VMEM((blocks, UPPER, traces), BF16),
            [pltpu.VMEM((blocks, rows, depth), BF16)] * PIECES,
            pltpu.VMEM((hops, slots, lat, traces), BF16),
            pltpu.VMEM((hops, slots, half, depth), BF16),
            pltpu.VMEM((hops, slots, UPPER, traces), BF16),
            pltpu.VMEM((PIECES, hops, slots, rows, depth), BF16),
            pltpu.VMEM((tiles, slots, lat, traces), BF16),
            pltpu.VMEM((tiles, slots, half, depth), BF16),
            pltpu.VMEM((tiles, 8, 128), jnp.int32),
            pltpu.SMEM((blocks,), jnp.int32),
            pltpu.SMEM((blocks,), jnp.int32),
            pltpu.SMEM((tiles, 8, 128), jnp.int32),
            pltpu.VMEM((2, lat, depth), F32),
            pltpu.VMEM((lat, depth), F32),
            dma((6,)), dma((8,)), dma((8,)), dma((6, 2)), dma((2, STOPS)),
            dma((hops,)), dma((hops,)), dma((hops,)), dma((hops,)), dma((1,)), dma((1,)),
            dma((PIECES,)), dma((PIECES,)), dma((hops,)), dma((hops,)), dma((PIECES, hops, 2)), dma((PIECES, hops, 2)),
            dma((4, 2)), dma((4, 2)), dma((1,)), dma((1,)),
        ],
        compiler_params=pltpu.CompilerParams(collective_id=0, has_side_effects=True, vmem_limit_bytes=60 << 20),
        cost_estimate=pl.CostEstimate(flops=10 << 30, bytes_accessed=12 << 20, transcendentals=0),
    )(residual_traces, time_weights, lateral_amplitude, intersection_tile.reshape(blocks), visit_stop)


def solution(mesh):
    assert mesh.shape["blk"] == 16 and mesh.shape["tile"] == 8
    in_specs = (
        P(("blk", "tile"), None),
        P(("blk", "tile"), None, None),
        P(("blk", "tile"), None, None),
        P(("blk", "tile"), None),
        P(("blk", "tile")),
    )
    out_specs = P(("blk", "tile"), None)
    return jax.shard_map(body, mesh=mesh, in_specs=in_specs, out_specs=out_specs, check_vma=False)
```

```python
import jax
import jax.numpy as jnp
from jax import lax
from jax.experimental import pallas as pl
from jax.experimental.pallas import tpu as pltpu
from jax.sharding import PartitionSpec as P

MESH = pl.DeviceIdType.MESH
MOST = 2
STOPS = 4
UPPER = 64
PIECES = 4
OFFSETS = (2, 1, 3)
CHUNK = 512
F32 = jnp.float32
BF16 = jnp.bfloat16


def kernel(r_hbm, w_hbm, a_hbm, tile_hbm, stop_hbm, out_ref, r_all, a_own, w_own, a_pair, w_pair, sa_own, sw_own, sa_pair,
           sw_pair, d_a, d_w, d_info, tile_ref, stop_ref, s_all, acc, part, loc, info_s, info_r, r_s, r_r, az_s, az_r, wz_s, wz_r,
           ap_s, ap_r, wp_s, wp_r, apz_s, apz_r, wpz_s, wpz_r, al_s, al_r, o_s, o_r):
    blk, tile = lax.axis_index("blk"), lax.axis_index("tile")
    groups, tiles = lax.axis_size("blk"), lax.axis_size("tile")
    zs = tiles // 2
    core, yh = blk % 2, (blk // 2) % 2
    z, h = tile // 2, tile % 2
    label = (h + yh) % 2
    blocks, lat = a_own.shape[0], a_own.shape[1]
    half = w_own.shape[1]
    rows = half // PIECES
    mine = pl.ds(pl.multiple_of(label * half, half), half)
    other = pl.ds(pl.multiple_of((1 - label) * half, half), half)

    pair = (blk, z * 2 + 1 - h)
    sibling = (blk + 1 - 2 * core, tile)
    next_chip = ((blk + 2) % groups, z * 2 + 1 - h)
    after_next = ((blk + 3) % groups, tile)
    drop = ((blk + groups - 1) % groups, z * 2 + 1 - h)
    is_b = (yh * core) == 0
    is_c = core == 1
    is_d = (yh * (1 - core)) == 1

    def remote(src, dst, send, recv, where):
        return pltpu.make_async_remote_copy(src_ref=src, dst_ref=dst, send_sem=send, recv_sem=recv, device_id=where,
                                            device_id_type=MESH)

    def lane_of(d):
        return (blk, ((z + d) % zs) * 2 + h)

    barrier = pltpu.get_barrier_semaphore()

    def greet(where):
        pl.semaphore_signal(barrier, inc=1, device_id=where, device_id_type=MESH)

    for j in range(1, 8):
        greet((blk, (tile + j) % tiles))
    greet(sibling)
    from_yh0_odd = (yh == 0) & (core == 1)

    @pl.when(from_yh0_odd)
    def _():
        greet(((blk + 1) % groups, z * 2 + 1 - h))

    @pl.when(jnp.logical_not(from_yh0_odd))
    def _():
        greet(((blk + groups - 2) % groups, z * 2 + 1 - h))

    @pl.when(core == 0)
    def _():
        greet(((blk + groups - 3) % groups, tile))

    cp_a = pltpu.make_async_copy(a_hbm, a_own, loc.at[0])
    cp_r = pltpu.make_async_copy(r_hbm.at[:, mine], r_all.at[h, 0], loc.at[1])
    cp_w = pltpu.make_async_copy(w_hbm.at[:, mine, :], w_own, loc.at[2])
    cp_tile = pltpu.make_async_copy(tile_hbm, tile_ref, loc.at[4])
    cp_stop = pltpu.make_async_copy(stop_hbm, stop_ref, loc.at[5])
    cp_tile.start()
    cp_stop.start()
    cp_a.start()
    cp_r.start()
    cp_w.start()

    lane = lax.broadcasted_iota(jnp.int32, d_info.shape[1:], 1)
    line = lax.broadcasted_iota(jnp.int32, d_info.shape[1:], 0)
    info = jnp.zeros(d_info.shape[1:], jnp.int32)
    cp_tile.wait()
    cp_stop.wait()
    targets = [tile_ref[b] for b in range(blocks)]
    slot_of = []
    for b in range(blocks):
        rank = sum([(targets[e] == targets[b]).astype(jnp.int32) for e in range(b)], jnp.int32(0))
        slot_of.append(targets[b] * MOST + rank)
        value = jnp.where(line == 0, b, jnp.where(line == 1, stop_ref[b], 1))
        info = jnp.where(lane == slot_of[b], value, info)
    d_info[tile] = info

    src_me = tile
    src_pair = z * 2 + 1 - h

    def pack(table, count, base, load, store):
        def one(r, carry):
            store(r, load(table(base + r)))
            return carry

        lax.fori_loop(0, count, one, 0)

    def own_block(slot):
        block = jnp.int32(0)
        for b in range(1, blocks):
            block = jnp.where(slot_of[b] == slot, b, block)
        return block

    def pair_block(slot):
        return s_all[src_pair, 0, slot]

    def base_of(d):
        return ((z + d) % zs) * (2 * MOST)

    def a_out(d):
        return remote(sa_own.at[d - 1], d_a.at[src_me], az_s.at[d - 1], az_r.at[d - 1], lane_of(d))

    cp_a.wait()
    for d in OFFSETS:
        def put(r, value, d=d):
            sa_own[d - 1, r] = value

        pack(own_block, 4, base_of(d), lambda b: a_own[b], put)

    pl.semaphore_wait(barrier, 8 + (1 - yh * core) + core + yh * (1 - core))

    def info_copy(j):
        return remote(d_info.at[tile], d_info.at[tile], info_s.at[j], info_r.at[j], (blk, (tile + j) % tiles))

    for j in range(1, 8):
        info_copy(j).start()

    r_pair = remote(r_hbm.at[:, other], r_all.at[h, 0], r_s.at[0, 0], r_r.at[h, 0], pair)
    a_over = remote(a_hbm.at[:, 0:UPPER, :], a_pair, ap_s.at[0], ap_r.at[0], pair)

    def w_over(i):
        at = pl.ds(pl.multiple_of((1 - label) * half + i * rows, rows), rows)
        return remote(w_hbm.at[:, at, :], w_pair[i], wp_s.at[i], wp_r.at[i], pair)

    r_pair.start()
    for d in OFFSETS:
        a_out(d).start()
    a_over.start()
    for i in range(PIECES):
        w_over(i).start()

    def hop(op, j, tau, k_from, k_to, where):
        return remote(r_all.at[tau, k_from], r_all.at[tau, k_to], r_s.at[op, j], r_r.at[tau, k_to], where)

    def taus(j):
        return h if j == 0 else 1 - h

    def op_a(j):
        return hop(1, j, taus(j), 0, 1, sibling)

    def op_b(j):
        return hop(2, j, taus(j), 0, 2, next_chip)

    def op_c(j):
        return hop(3, j, taus(j), 0, 3, after_next)

    def op_d(j):
        return hop(4, j, taus(j), 3, 2, drop)

    def op_e0(j):
        return hop(5, j, taus(j), 2, 3, sibling)

    def op_e1(j):
        return hop(5, j, taus(j), 2, 1, sibling)

    def got_r(tau, k):
        remote(r_all.at[tau, k], r_all.at[tau, k], r_s.at[0, 0], r_r.at[tau, k], pair).wait_recv()

    def spread(j):
        @pl.when(is_c)
        def _():
            op_c(j).start()

        @pl.when(is_b)
        def _():
            op_b(j).start()

        @pl.when(core == 0)
        def _():
            op_a(j).start()

    def forward(j):
        got_r(taus(j), 2)

        @pl.when(core == 0)
        def _():
            op_e0(j).start()

        @pl.when(core == 1)
        def _():
            op_e1(j).start()

    def arrive_3(j):
        got_r(taus(j), 3)

        @pl.when(is_d)
        def _():
            op_d(j).start()

    cp_r.wait()
    spread(0)

    def w_out(d):
        return remote(sw_own.at[d - 1], d_w.at[src_me], wz_s.at[d - 1], wz_r.at[d - 1], lane_of(d))

    def put_a(r, value):
        d_a[src_me, r] = value

    pack(own_block, 4, base_of(0), lambda b: a_own[b], put_a)

    def source(d, flip):
        return ((z + zs - d) % zs) * 2 + (1 - h if flip else h)

    lows = [(d, t, 0, MOST) for t in range(2) for d in range(4)]
    lows[-1:] = [(3, 1, i, 1) for i in range(MOST)]

    def low_at(src, tau, skip, count):
        return d_a.at[src, pl.ds(tau * MOST + skip, count), UPPER:lat, :]

    def low(n):
        d, t, skip, count = lows[n]
        at = low_at(source(d, False), h if t == 0 else 1 - h, skip, count)
        return remote(at, at, al_s.at[n], al_r.at[n], pair)

    cp_w.wait()
    for d in OFFSETS:
        def put(r, value, d=d):
            sw_own[d - 1, r] = value

        pack(own_block, 4, base_of(d), lambda b: w_own[b], put)
        w_out(d).start()

    def put_w(r, value):
        d_w[src_me, r] = value

    pack(own_block, 4, base_of(0), lambda b: w_own[b], put_w)

    for j in range(1, 8):
        src = (tile + tiles - j) % tiles
        remote(d_info.at[src], d_info.at[src], info_s.at[j], info_r.at[j], pair).wait_recv()
    cp_all = pltpu.make_async_copy(d_info, s_all, loc.at[3])
    cp_all.start()
    cp_all.wait()

    got_r(1 - h, 0)
    spread(1)

    def ap_out(d):
        return remote(sa_pair.at[d - 1], d_a.at[src_pair, :, 0:UPPER, :], apz_s.at[d - 1], apz_r.at[d - 1], lane_of(d))

    def wp_out(i, d, t):
        two = pl.ds((1 - h if t == 0 else h) * MOST, MOST)
        return remote(sw_pair.at[i, d - 1, two], d_w.at[src_pair, two, pl.ds(i * rows, rows), :], wpz_s.at[i, d - 1, t],
                      wpz_r.at[i, d - 1, t], lane_of(d))

    a_over.wait_recv()
    for d in OFFSETS:
        def put(r, value, d=d):
            sa_pair[d - 1, r] = value

        pack(pair_block, 4, base_of(d), lambda b: a_pair[b], put)
        ap_out(d).start()

    def put_ap(r, value):
        d_a[src_pair, r, 0:UPPER, :] = value

    pack(pair_block, 4, base_of(0), lambda b: a_pair[b], put_ap)

    def relay_piece(i, t):
        skip = (1 - h if t == 0 else h) * MOST
        for d in OFFSETS:
            def put(r, value, d=d):
                sw_pair[i, d - 1, skip + r] = value

            pack(pair_block, MOST, base_of(d) + skip, lambda b: w_pair[i][b], put)
            wp_out(i, d, t).start()

        def put_wp(r, value):
            d_w[src_pair, skip + r, i * rows:(i + 1) * rows, :] = value

        pack(pair_block, MOST, base_of(0) + skip, lambda b: w_pair[i][b], put_wp)

    def got_own_a(d):
        src = source(d, False)
        remote(d_a.at[src], d_a.at[src], az_s.at[d - 1], az_r.at[d - 1], pair).wait_recv()

    for d in (1, 3, 2):
        got_own_a(d)
    for n in range(len(lows)):
        low(n).start()

    @pl.when(core == 0)
    def _():
        arrive_3(0)

    forward(1)
    for i in range(PIECES):
        w_over(i).wait_recv()
        relay_piece(i, 0)
        if i == PIECES // 2 - 1:
            @pl.when(core == 0)
            def _():
                arrive_3(1)

    for i in range(PIECES):
        relay_piece(i, 1)
    forward(0)

    got_r(0, 1)
    got_r(1, 1)

    @pl.when(core == 1)
    def _():
        got_r(0, 3)
        got_r(1, 3)

    acc[...] = jnp.zeros_like(acc)
    first = z * (2 * MOST)

    def facts(src, r):
        return s_all[src, 1, first + r], s_all[src, 2, first + r].astype(F32)

    def chunk_q(src, r, k, n):
        return jnp.dot(d_a[src, r], r_all[r // MOST, k, :, n * CHUNK:(n + 1) * CHUNK],
                       preferred_element_type=F32).astype(BF16)

    def whole(src, begin, count):
        def one(r, carry):
            k, filled = facts(src, r)
            total = jnp.zeros(acc.shape[1:], F32)
            for n in range(half // CHUNK):
                total += jnp.dot(chunk_q(src, r, k, n), d_w[src, r, n * CHUNK:(n + 1) * CHUNK, :],
                                 preferred_element_type=F32)
            acc[r // MOST] += filled * total
            return carry

        lax.fori_loop(begin, begin + count, one, 0)

    def front(src, d, begin, count):
        def one(r, carry):
            k, _ = facts(src, r)
            for n in range(half // CHUNK):
                sa_own[d - 1, r, :, n * CHUNK:(n + 1) * CHUNK] = chunk_q(src, r, k, n)
            return carry

        lax.fori_loop(begin, begin + count, one, 0)

    def back(src, d, begin, low_row, high_row):
        def one(r, carry):
            _, filled = facts(src, r)
            acc[r // MOST] += filled * jnp.dot(sa_own[d - 1, r, :, low_row:high_row], d_w[src, r, low_row:high_row, :],
                                               preferred_element_type=F32)
            return carry

        lax.fori_loop(begin, begin + MOST, one, 0)

    whole(src_me, 0, 2 * MOST)
    for d in (1, 3, 2):
        src = source(d, False)
        remote(d_w.at[src], d_w.at[src], wz_s.at[d - 1], wz_r.at[d - 1], pair).wait_recv()
        whole(src, 0, 2 * MOST)
    for d in OFFSETS:
        a_out(d).wait_send()
    for d in OFFSETS:
        at = d_a.at[source(d, True), :, 0:UPPER, :]
        remote(at, at, apz_s.at[d - 1], apz_r.at[d - 1], pair).wait_recv()

    home = remote(acc.at[1 - h], part, o_s.at[0], o_r.at[0], pair)
    last = half - rows
    for t in range(2):
        tau = 1 - h if t == 0 else h
        begin = tau * MOST

        def got_low(n):
            d, _, skip, count = lows[n]
            at = low_at(source(d, True), tau, skip, count)
            remote(at, at, al_s.at[n], al_r.at[n], pair).wait_recv()

        def got_w(d, i):
            at = d_w.at[source(d, True), pl.ds(begin, MOST), pl.ds(i * rows, rows), :]
            remote(at, at, wpz_s.at[i, d - 1, t], wpz_r.at[i, d - 1, t], pair).wait_recv()

        got_low(4 * t)
        whole(src_pair, begin, MOST)
        for d in (1, 2, 3):
            for n in range(4 * t, len(lows)):
                if lows[n][:2] == (d, t):
                    got_low(n)
                    front(source(d, True), d, begin + lows[n][2], lows[n][3])
            for i in range(PIECES - 1):
                got_w(d, i)
            back(source(d, True), d, begin, 0, last)
        for d in OFFSETS:
            got_w(d, PIECES - 1)
            back(source(d, True), d, begin, last, half)
        if t == 0:
            home.start()
            for j in range(1, 8):
                info_copy(j).wait_send()
            r_pair.wait_send()
            a_over.wait_send()
            for i in range(PIECES):
                w_over(i).wait_send()
            for d in OFFSETS:
                w_out(d).wait_send()
                ap_out(d).wait_send()
                for i in range(PIECES):
                    wp_out(i, d, 0).wait_send()
            for d in range(4):
                low(d).wait_send()
            for j in range(2):
                @pl.when(is_c)
                def _():
                    op_c(j).wait_send()

                @pl.when(is_b)
                def _():
                    op_b(j).wait_send()

                @pl.when(is_d)
                def _():
                    op_d(j).wait_send()

                @pl.when(core == 0)
                def _():
                    op_a(j).wait_send()
                    op_e0(j).wait_send()

                @pl.when(core == 1)
                def _():
                    op_e1(j).wait_send()


    for d in OFFSETS:
        for i in range(PIECES):
            wp_out(i, d, 1).wait_send()
    for n in range(4, len(lows)):
        low(n).wait_send()
    home.wait()
    out_ref[...] = acc[h] + part[...]


def body(residual_traces, time_weights, lateral_amplitude, intersection_tile, visit_stop):
    traces, samples = residual_traces.shape
    blocks, _, depth = time_weights.shape
    lat = lateral_amplitude.shape[1]
    tiles = lax.axis_size("tile")
    half, slots = samples // 2, 2 * MOST
    rows = half // PIECES
    hops = tiles // 2 - 1
    dma = pltpu.SemaphoreType.DMA
    return pl.pallas_call(
        kernel,
        out_shape=jax.ShapeDtypeStruct((lat, depth), F32),
        in_specs=[pl.BlockSpec(memory_space=pl.ANY)] * 5,
        out_specs=pl.BlockSpec(memory_space=pltpu.VMEM),
        scratch_shapes=[
            pltpu.VMEM((2, STOPS, traces, half), BF16),
            pltpu.VMEM((blocks, lat, traces), BF16),
            pltpu.VMEM((blocks, half, depth), BF16),
            pltpu.VMEM((blocks, UPPER, traces), BF16),
            [pltpu.VMEM((blocks, rows, depth), BF16)] * PIECES,
            pltpu.VMEM((hops, slots, lat, traces), BF16),
            pltpu.VMEM((hops, slots, half, depth), BF16),
            pltpu.VMEM((hops, slots, UPPER, traces), BF16),
            pltpu.VMEM((PIECES, hops, slots, rows, depth), BF16),
            pltpu.VMEM((tiles, slots, lat, traces), BF16),
            pltpu.VMEM((tiles, slots, half, depth), BF16),
            pltpu.VMEM((tiles, 8, 128), jnp.int32),
            pltpu.SMEM((blocks,), jnp.int32),
            pltpu.SMEM((blocks,), jnp.int32),
            pltpu.SMEM((tiles, 8, 128), jnp.int32),
            pltpu.VMEM((2, lat, depth), F32),
            pltpu.VMEM((lat, depth), F32),
            dma((6,)), dma((8,)), dma((8,)), dma((6, 2)), dma((2, STOPS)),
            dma((hops,)), dma((hops,)), dma((hops,)), dma((hops,)), dma((1,)), dma((1,)),
            dma((PIECES,)), dma((PIECES,)), dma((hops,)), dma((hops,)), dma((PIECES, hops, 2)), dma((PIECES, hops, 2)),
            dma((9,)), dma((9,)), dma((1,)), dma((1,)),
        ],
        compiler_params=pltpu.CompilerParams(collective_id=0, has_side_effects=True, vmem_limit_bytes=60 << 20),
        cost_estimate=pl.CostEstimate(flops=10 << 30, bytes_accessed=12 << 20, transcendentals=0),
    )(residual_traces, time_weights, lateral_amplitude, intersection_tile.reshape(blocks), visit_stop)


def solution(mesh):
    assert mesh.shape["blk"] == 16 and mesh.shape["tile"] == 8
    in_specs = (
        P(("blk", "tile"), None),
        P(("blk", "tile"), None, None),
        P(("blk", "tile"), None, None),
        P(("blk", "tile"), None),
        P(("blk", "tile")),
    )
    out_specs = P(("blk", "tile"), None)
    return jax.shard_map(body, mesh=mesh, in_specs=in_specs, out_specs=out_specs, check_vma=False)
```
